32 devices in a mesh: grp: 4 (over y, core), dev: 8 (over z, x).
Axes of the slice: x: 2, y: 2, z: 4, core: 2. Of those that a mesh axis runs over, the one named last changes fastest.
Arguments:
- voltage_real: bfloat16 [2048, 110592], P(('grp', 'dev')), may hold values from -6 to 6
- voltage_imaginary: bfloat16 [2048, 110592], P(('grp', 'dev')), may hold values from -6 to 6
- filter_taps: float32 [16, 4096], replicated, may hold values from -1.5 to 1.5
- weights_re: float32 [8, 2048, 512], P('dev'), may hold values from -0.0625 to 0.0625
- weights_im: float32 [8, 2048, 512], P('dev'), may hold values from -0.0625 to 0.0625
- owners: int32 [2], replicated, may hold values from 0 to 7
- antenna_map: int32 [2048], replicated, may hold values from 0 to 2047, each once
Outputs:
- beam_power: float32 [2, 4096, 512], P(None, ('grp', 'dev'))
The draws below stay inside these ranges and needn't reach their ends.
Inputs may be any that keep to these rules, and one draw needn't show every extreme that they name: `owners`: the index along dev of the device whose calibration serves each step. A permutation: voltage slot j carries antenna antenna_map[j].
All inputs are finite; a program needn't handle non-finite values.
Results may differ from the reference program's by a relative error of at most 0.0022.
Values may be sent and summed in bfloat16 or wider, within the bound.
A program may use at most 256 MiB of HBM per device.

```python
import jax
import jax.numpy as jnp
from jax import lax

A = 2048
FREQ_CHANNELS = 4096
B = 512
TAPS = 16
SPECTRA_PER_STEP = 6
STEPS = 2
SAMPLES = 110592
N_DEV = 8


def steps_of(key, shape, split, least, top_value):
    loudness = 1.0
    for axis_at, shards_of in split:
        steps = jax.random.uniform(jax.random.fold_in(jax.random.fold_in(key, 6), axis_at), (shards_of,), jnp.float32, least / len(split), top_value / len(split))
        loudness = loudness * jnp.repeat(jnp.exp(steps), shape[axis_at] // shards_of).reshape((-1,) + (1,) * (len(shape) - 1 - axis_at))
    return loudness


def bell_draw(own_key, extent, scale, limit, cuts=(), kind=jnp.bfloat16):
    factor_of = steps_of(own_key, extent, cuts, -0.22, 0.18) if cuts else 1.0
    result = jax.random.normal(own_key, extent, jnp.float32) * scale * factor_of
    return jnp.minimum(jnp.maximum(result, -limit), limit).astype(kind)


def setup_inputs(seed: int = 0) -> dict:
    seeds = jax.random.split(jax.random.key(seed), 8)
    return {
        "voltage_real": bell_draw(seeds[0], (A, SAMPLES), 1.0, 6.0, ((0, 32),)),
        "voltage_imaginary": bell_draw(seeds[1], (A, SAMPLES), 1.0, 6.0, ((0, 32),)),
        "filter_taps": bell_draw(seeds[2], (TAPS, FREQ_CHANNELS), 0.25, 1.5, (), jnp.float32),
        "weights_re": bell_draw(seeds[3], (N_DEV, A, B), (4 * A) ** -0.5, 0.0625, ((0, 8),), jnp.float32),
        "weights_im": bell_draw(seeds[4], (N_DEV, A, B), (4 * A) ** -0.5, 0.0625, ((0, 8),), jnp.float32),
        "owners": jax.random.randint(seeds[5], (STEPS,), 0, N_DEV).astype(jnp.int32),
        "antenna_map": jax.random.permutation(seeds[6], A).astype(jnp.int32),
    }


def spectra_block(pieces, filter_taps, offset):
    blocks_re, blocks_im = pieces
    frames_re = jnp.zeros((blocks_re.shape[0], SPECTRA_PER_STEP, FREQ_CHANNELS), jnp.float32)
    frames_im = jnp.zeros((blocks_re.shape[0], SPECTRA_PER_STEP, FREQ_CHANNELS), jnp.float32)
    for tap_index in range(TAPS):
        lower = offset + tap_index
        frames_re = frames_re + blocks_re[:, lower:lower + SPECTRA_PER_STEP].astype(jnp.float32) * filter_taps[tap_index]
        frames_im = frames_im + blocks_im[:, lower:lower + SPECTRA_PER_STEP].astype(jnp.float32) * filter_taps[tap_index]
    spectrum_rows = jnp.fft.fft(frames_re + 1j * frames_im, axis=-1) * (FREQ_CHANNELS ** -0.5)
    return jnp.real(spectrum_rows).astype(jnp.bfloat16), jnp.imag(spectrum_rows).astype(jnp.bfloat16)


def reference(voltage_real, voltage_imaginary, filter_taps, weights_re, weights_im, owners, antenna_map):
    width = min(A, 256)
    count = A // width
    blocks_re = voltage_real.reshape(count, width, -1, FREQ_CHANNELS)
    blocks_im = voltage_imaginary.reshape(count, width, -1, FREQ_CHANNELS)
    col_width = min(FREQ_CHANNELS, 256)
    results = []
    for window_step in range(STEPS):
        offset = window_step * SPECTRA_PER_STEP

        def make_block(pieces):
            return spectra_block(pieces, filter_taps, offset)

        spectrum_real, spectrum_imaginary = lax.map(make_block, (blocks_re, blocks_im))
        stacked = jnp.concatenate([spectrum_real.reshape(A, SPECTRA_PER_STEP, FREQ_CHANNELS), spectrum_imaginary.reshape(A, SPECTRA_PER_STEP, FREQ_CHANNELS)], 0)
        leader = owners[window_step]
        cal_re = jnp.take(weights_re[leader].astype(jnp.bfloat16), antenna_map, axis=0)
        cal_im = jnp.take(weights_im[leader].astype(jnp.bfloat16), antenna_map, axis=0)
        mixing = jnp.concatenate([jnp.concatenate([cal_re, cal_im], 1), jnp.concatenate([-cal_im, cal_re], 1)], 0).astype(jnp.float32)

        def detect_block(block_index):
            start_channel = (block_index * col_width).astype(jnp.int32)
            column_part = lax.dynamic_slice_in_dim(stacked, start_channel, col_width, 2).astype(jnp.float32)
            beam_terms = jnp.einsum('atf,ab->tfb', column_part, mixing, precision=lax.Precision.HIGHEST)
            return jnp.mean(beam_terms[..., :B] ** 2 + beam_terms[..., B:] ** 2, axis=0)

        beam_power = lax.map(detect_block, jnp.arange(FREQ_CHANNELS // col_width, dtype=jnp.int32))
        results.append(beam_power.reshape(FREQ_CHANNELS, B))
    return jnp.stack(results)
```

```python
import functools
import math

import jax
import jax.numpy as jnp
import ml_dtypes
import numpy as np
from jax import lax
from jax.experimental import pallas as pl
from jax.experimental.pallas import tpu as pltpu
from jax.sharding import PartitionSpec as P

FREQ_CHANNELS = 4096
TAPS = 16
SPECTRA_PER_STEP = 6
STEPS = 2
LANES = 128
OUTER = FREQ_CHANNELS // LANES
ANT_BLOCK = 16


def dft_tables():
    f1 = np.arange(OUTER)[:, None, None]
    f2 = np.arange(LANES)[None, :, None]
    n2 = np.arange(LANES)[None, None, :]
    angle = (n2 * (f1 + OUTER * f2) % FREQ_CHANNELS) * (2.0 * math.pi / FREQ_CHANNELS)
    c = np.cos(angle) / math.sqrt(FREQ_CHANNELS)
    s = np.sin(angle) / math.sqrt(FREQ_CHANNELS)
    real = np.concatenate([c, s], -1).reshape(OUTER, OUTER, 4, 2 * LANES)
    imag = np.concatenate([-s, c], -1).reshape(OUTER, OUTER, 4, 2 * LANES)
    odd = (np.arange(OUTER) % 2 == 1)[:, None, None, None]
    first = np.where(odd, imag, real)
    second = np.where(odd, real, imag)
    table = np.stack([first, second], 2).reshape(OUTER, 2 * LANES, 2 * LANES)
    high = table.astype(ml_dtypes.bfloat16)
    low = (table - high.astype(np.float64)).astype(ml_dtypes.bfloat16)
    return high, low


def rotate(value, k, length):
    re, im = value
    k = k % length
    if k == 0:
        return re, im
    if 4 * k == length:
        return im, -re
    if 2 * k == length:
        return -re, -im
    if 4 * k == 3 * length:
        return -im, re
    c, s = math.cos(2 * math.pi * k / length), math.sin(2 * math.pi * k / length)
    if 8 * k == length:
        return (re + im) * c, (im - re) * c
    if 8 * k == 3 * length:
        return (im - re) * s, (re + im) * (-s)
    return re * c + im * s, im * c - re * s


def small_fft(values):
    count = len(values)
    if count == 1:
        return values
    even = small_fft(values[0::2])
    odd = small_fft(values[1::2])
    low, high = [], []
    for k in range(count // 2):
        a = even[k]
        b = rotate(odd[k], k, count)
        low.append((a[0] + b[0], a[1] + b[1]))
        high.append((a[0] - b[0], a[1] - b[1]))
    return low + high


def channelize_kernel(step, ants, vr_ref, vi_ref, taps_ref, wh_ref, wl_ref, out_ref, fr_ref, fi_ref, xs_ref):
    block = pl.program_id(0)
    offset = step * SPECTRA_PER_STEP

    @pl.loop(0, OUTER)
    def _(n1):
        lane = pl.multiple_of(n1 * LANES, LANES)
        taps = [jnp.broadcast_to(taps_ref[k : k + 1, pl.ds(lane, LANES)], (8, LANES)) for k in range(TAPS)]
        for v_ref, f_ref in ((vr_ref, fr_ref), (vi_ref, fi_ref)):
            acc = [[None, None] for _ in range(SPECTRA_PER_STEP)]
            for b in range(SPECTRA_PER_STEP + TAPS - 1):
                start = pl.multiple_of((offset + b) * FREQ_CHANNELS + lane, LANES)
                value = v_ref[:, pl.ds(start, LANES)].astype(jnp.float32)
                for h in range(2):
                    half = value[8 * h : 8 * h + 8]
                    for t in range(SPECTRA_PER_STEP):
                        k = b - t
                        if 0 <= k < TAPS:
                            term = half * taps[k]
                            acc[t][h] = term if acc[t][h] is None else acc[t][h] + term
            for t in range(SPECTRA_PER_STEP):
                for h in range(2):
                    f_ref[t, h, n1] = acc[t][h]

    @pl.loop(0, SPECTRA_PER_STEP)
    def _(t):
        for h in range(2):
            values = [(fr_ref[t, h, n1], fi_ref[t, h, n1]) for n1 in range(OUTER)]
            result = small_fft(values)
            row = pl.multiple_of(t * ants + block * ANT_BLOCK + 8 * h, 8)
            for f1 in range(OUTER):
                xs_ref[f1, pl.ds(row, 8), 0:LANES] = result[f1][0]
                xs_ref[f1, pl.ds(row, 8), LANES : 2 * LANES] = result[f1][1]

    @pl.when(block == pl.num_programs(0) - 1)
    def _():
        columns = SPECTRA_PER_STEP * ants
        nt = functools.partial(
            lax.dot_general,
            dimension_numbers=(((1,), (1,)), ((), ())),
            preferred_element_type=jnp.float32,
        )

        @pl.loop(0, OUTER // 2)
        def _(pair):
            parts = []
            for lo in range(2):
                f1 = 2 * pair + lo
                x = xs_ref[f1]
                xh = x.astype(jnp.bfloat16)
                xl = (x - xh.astype(jnp.float32)).astype(jnp.bfloat16)
                wh = wh_ref[f1]
                y = nt(wh, xh) + nt(wl_ref[f1], xh) + nt(wh, xl)
                parts.append(y.reshape(OUTER, 8, columns))
            a, b = parts
            top = lax.broadcasted_iota(jnp.int32, (OUTER, 8, columns), 1) < 4
            re = jnp.where(top, a, b)
            im = pltpu.roll(jnp.where(top, b, a), 4, 1)
            out_ref[:, pair] = jnp.concatenate([re, im], 1).astype(jnp.bfloat16)


def channelize(step, voltage_real, voltage_imaginary, filter_taps, high, low):
    ants, samples = voltage_real.shape
    columns = SPECTRA_PER_STEP * ants
    once = pl.Buffered(1)
    stream = pl.BlockSpec((ANT_BLOCK, samples), lambda i: (i, 0))
    table = pl.BlockSpec((OUTER, 2 * LANES, 2 * LANES), lambda i: (0, 0, 0), pipeline_mode=once)
    return pl.pallas_call(
        functools.partial(channelize_kernel, step, ants),
        grid=(ants // ANT_BLOCK,),
        in_specs=[
            stream,
            stream,
            pl.BlockSpec((TAPS, FREQ_CHANNELS), lambda i: (0, 0), pipeline_mode=once),
            table,
            table,
        ],
        out_specs=pl.BlockSpec((OUTER, 16, 16, columns), lambda i: (0, 0, 0, 0), pipeline_mode=once),
        out_shape=jax.ShapeDtypeStruct((OUTER, 16, 16, columns), jnp.bfloat16),
        scratch_shapes=[
            pltpu.VMEM((SPECTRA_PER_STEP, 2, OUTER, 8, LANES), jnp.float32),
            pltpu.VMEM((SPECTRA_PER_STEP, 2, OUTER, 8, LANES), jnp.float32),
            pltpu.VMEM((OUTER, columns, 2 * LANES), jnp.float32),
        ],
        compiler_params=pltpu.CompilerParams(vmem_limit_bytes=56 * 2**20),
        cost_estimate=pl.CostEstimate(
            flops=20_000_000_000, bytes_accessed=50_000_000, transcendentals=0
        ),
        name="channelize",
    )(voltage_real, voltage_imaginary, filter_taps, high, low)


def detect_kernel(sources, ants, x_ref, w_ref, out_ref, xs_ref):
    rows = x_ref.shape[1]
    for t in range(SPECTRA_PER_STEP):
        for pair in range(sources // 2):
            xs_ref[t * rows : (t + 1) * rows, 2 * pair * ants : 2 * (pair + 1) * ants] = jnp.concatenate(
                [x_ref[2 * pair + j, :, t * ants : (t + 1) * ants] for j in range(2)], 1
            )
    beams = w_ref.shape[1] // 2
    total = None
    for t in range(SPECTRA_PER_STEP):
        g = jnp.dot(xs_ref[t * rows : (t + 1) * rows], w_ref[...], preferred_element_type=jnp.float32)
        g = g.reshape(rows // 16, 2, 8, 2 * beams)
        re, im = g[:, 0], g[:, 1]
        beam_re = re[..., :beams] - im[..., beams:]
        beam_im = re[..., beams:] + im[..., :beams]
        power = beam_re * beam_re + beam_im * beam_im
        total = power if total is None else total + power
    out_ref[...] = (total * (1.0 / SPECTRA_PER_STEP)).reshape(rows // 2, beams)


def detect(received, weights, sources):
    rows, columns = received.shape[1], received.shape[2]
    ants = columns // SPECTRA_PER_STEP
    beams = weights.shape[1] // 2
    block = rows // 2
    power = pl.pallas_call(
        functools.partial(detect_kernel, sources, ants),
        grid=(2,),
        in_specs=[
            pl.BlockSpec((sources, block, columns), lambda i: (0, i, 0)),
            pl.BlockSpec(weights.shape, lambda i: (0, 0), pipeline_mode=pl.Buffered(1)),
        ],
        out_specs=pl.BlockSpec((block // 2, beams), lambda i: (i, 0)),
        out_shape=jax.ShapeDtypeStruct((rows // 2, beams), jnp.float32),
        scratch_shapes=[pltpu.VMEM((SPECTRA_PER_STEP * block, sources * ants), jnp.bfloat16)],
        compiler_params=pltpu.CompilerParams(vmem_limit_bytes=48 * 2**20),
        cost_estimate=pl.CostEstimate(flops=6_500_000_000, bytes_accessed=11_000_000, transcendentals=0),
        name="detect",
    )(received, weights)
    return power.reshape(OUTER, 4, beams).swapaxes(0, 1).reshape(rows // 2, beams)


def detect_any(received, weights, sources, owned):
    ants = received.shape[-1]
    beams = weights.shape[1] // 2
    rows = received.transpose(4, 1, 3, 5, 2, 0, 6).reshape(
        OUTER * owned, SPECTRA_PER_STEP, 2, sources * ants
    )
    terms = jnp.einsum("ftpa,ab->ftpb", rows, weights, preferred_element_type=jnp.float32)
    beam_re = terms[:, :, 0, :beams] - terms[:, :, 1, beams:]
    beam_im = terms[:, :, 0, beams:] + terms[:, :, 1, :beams]
    return jnp.mean(beam_re**2 + beam_im**2, axis=1)


def on_device(groups, members, vr, vi, filter_taps, weights_re, weights_im, owners, antenna_map):
    devices = groups * members
    ants = vr.shape[0]
    total_ants = antenna_map.shape[0]
    quarter = total_ants // groups
    rows = lax.dynamic_slice_in_dim(antenna_map, lax.axis_index("grp") * quarter, quarter)
    own = jnp.concatenate(
        [
            jnp.take(weights_re[0], rows, axis=0).astype(jnp.bfloat16),
            jnp.take(weights_im[0], rows, axis=0).astype(jnp.bfloat16),
        ],
        1,
    )
    mine = lax.axis_index("dev") == owners
    kept = jnp.where(mine[:, None, None], own[None], 0).astype(jnp.bfloat16)
    weights = lax.all_gather(lax.psum(kept, "dev"), "grp", axis=1, tiled=True)

    high, low = (jnp.asarray(table) for table in dft_tables())
    owned = LANES // devices
    sent = []
    for step in range(STEPS):
        spectra = channelize(step, vr, vi, filter_taps, high, low)
        if devices != OUTER:
            spectra = spectra.reshape(OUTER, 16, 2, 2, 4 // owned, owned, SPECTRA_PER_STEP * ants)
            spectra = spectra.transpose(0, 4, 1, 2, 3, 5, 6)
        spectra = spectra.reshape(devices, -1, SPECTRA_PER_STEP * ants)
        sent.append(lax.all_to_all(spectra, ("grp", "dev"), split_axis=0, concat_axis=0, tiled=True))
    outputs = []
    for step in range(STEPS):
        if devices == OUTER:
            outputs.append(detect(sent[step], weights[step], devices))
        else:
            received = sent[step].reshape(devices, 16, 2, 2, owned, SPECTRA_PER_STEP, ants)
            outputs.append(detect_any(received, weights[step], devices, owned))
    return jnp.stack(outputs)


def solution(mesh):
    groups, members = mesh.shape["grp"], mesh.shape["dev"]
    return jax.shard_map(
        functools.partial(on_device, groups, members),
        mesh=mesh,
        in_specs=(
            P(("grp", "dev"), None),
            P(("grp", "dev"), None),
            P(),
            P("dev", None, None),
            P("dev", None, None),
            P(),
            P(),
        ),
        out_specs=P(None, ("grp", "dev"), None),
        check_vma=False,
    )
```

```python
import functools
import math

import jax
import jax.numpy as jnp
import ml_dtypes
import numpy as np
from jax import lax
from jax.experimental import pallas as pl
from jax.experimental.pallas import tpu as pltpu
from jax.sharding import PartitionSpec as P

FREQ_CHANNELS = 4096
TAPS = 16
SPECTRA_PER_STEP = 6
STEPS = 2
LANES = 128
OUTER = FREQ_CHANNELS // LANES
ANT_BLOCK = 16


def dft_tables():
    f1 = np.arange(OUTER)[:, None, None]
    f2 = np.arange(LANES)[None, :, None]
    n2 = np.arange(LANES)[None, None, :]
    angle = (n2 * (f1 + OUTER * f2) % FREQ_CHANNELS) * (2.0 * math.pi / FREQ_CHANNELS)
    c = np.cos(angle) / math.sqrt(FREQ_CHANNELS)
    s = np.sin(angle) / math.sqrt(FREQ_CHANNELS)
    real = np.concatenate([c, s], -1).reshape(OUTER, OUTER, 4, 2 * LANES)
    imag = np.concatenate([-s, c], -1).reshape(OUTER, OUTER, 4, 2 * LANES)
    odd = (np.arange(OUTER) % 2 == 1)[:, None, None, None]
    first = np.where(odd, imag, real)
    second = np.where(odd, real, imag)
    table = np.stack([first, second], 2).reshape(OUTER, 2 * LANES, 2 * LANES)
    high = table.astype(ml_dtypes.bfloat16)
    low = (table - high.astype(np.float64)).astype(ml_dtypes.bfloat16)
    return high, low


def rotate(value, k, length):
    re, im = value
    k = k % length
    if k == 0:
        return re, im
    if 4 * k == length:
        return im, -re
    if 2 * k == length:
        return -re, -im
    if 4 * k == 3 * length:
        return -im, re
    c, s = math.cos(2 * math.pi * k / length), math.sin(2 * math.pi * k / length)
    if 8 * k == length:
        return (re + im) * c, (im - re) * c
    if 8 * k == 3 * length:
        return (im - re) * s, (re + im) * (-s)
    return re * c + im * s, im * c - re * s


def small_fft(values):
    count = len(values)
    if count == 1:
        return values
    even = small_fft(values[0::2])
    odd = small_fft(values[1::2])
    low, high = [], []
    for k in range(count // 2):
        a = even[k]
        b = rotate(odd[k], k, count)
        low.append((a[0] + b[0], a[1] + b[1]))
        high.append((a[0] - b[0], a[1] - b[1]))
    return low + high


def channelize_kernel(step, ants, vr_ref, vi_ref, taps_ref, wh_ref, wl_ref, out_ref, fr_ref, fi_ref, xs_ref):
    block = pl.program_id(0)
    offset = step * SPECTRA_PER_STEP

    @pl.loop(0, OUTER)
    def _(n1):
        lane = pl.multiple_of(n1 * LANES, LANES)
        taps = [jnp.broadcast_to(taps_ref[k : k + 1, pl.ds(lane, LANES)], (8, LANES)) for k in range(TAPS)]
        for v_ref, f_ref in ((vr_ref, fr_ref), (vi_ref, fi_ref)):
            acc = [[None, None] for _ in range(SPECTRA_PER_STEP)]
            for b in range(SPECTRA_PER_STEP + TAPS - 1):
                start = pl.multiple_of((offset + b) * FREQ_CHANNELS + lane, LANES)
                value = v_ref[:, pl.ds(start, LANES)].astype(jnp.float32)
                for h in range(2):
                    half = value[8 * h : 8 * h + 8]
                    for t in range(SPECTRA_PER_STEP):
                        k = b - t
                        if 0 <= k < TAPS:
                            term = half * taps[k]
                            acc[t][h] = term if acc[t][h] is None else acc[t][h] + term
            for t in range(SPECTRA_PER_STEP):
                for h in range(2):
                    f_ref[t, h, n1] = acc[t][h]

    @pl.loop(0, SPECTRA_PER_STEP)
    def _(t):
        for h in range(2):
            values = [(fr_ref[t, h, n1], fi_ref[t, h, n1]) for n1 in range(OUTER)]
            result = small_fft(values)
            row = pl.multiple_of(t * ants + block * ANT_BLOCK + 8 * h, 8)
            for f1 in range(OUTER):
                xs_ref[f1, pl.ds(row, 8), 0:LANES] = result[f1][0]
                xs_ref[f1, pl.ds(row, 8), LANES : 2 * LANES] = result[f1][1]

    @pl.when(block == pl.num_programs(0) - 1)
    def _():
        columns = SPECTRA_PER_STEP * ants
        nt = functools.partial(
            lax.dot_general,
            dimension_numbers=(((1,), (1,)), ((), ())),
            preferred_element_type=jnp.float32,
        )

        @pl.loop(0, OUTER // 2)
        def _(pair):
            parts = []
            for lo in range(2):
                f1 = 2 * pair + lo
                x = xs_ref[f1]
                xh = x.astype(jnp.bfloat16)
                xl = (x - xh.astype(jnp.float32)).astype(jnp.bfloat16)
                wh = wh_ref[f1]
                y = nt(wh, xh) + nt(wl_ref[f1], xh) + nt(wh, xl)
                parts.append(y.reshape(OUTER, 8, columns))
            a, b = parts
            top = lax.broadcasted_iota(jnp.int32, (OUTER, 8, columns), 1) < 4
            re = jnp.where(top, a, b)
            im = pltpu.roll(jnp.where(top, b, a), 4, 1)
            out_ref[:, pair] = jnp.concatenate([re, im], 1).astype(jnp.bfloat16)


def channelize(step, voltage_real, voltage_imaginary, filter_taps, high, low):
    ants, samples = voltage_real.shape
    columns = SPECTRA_PER_STEP * ants
    once = pl.Buffered(1)
    stream = pl.BlockSpec((ANT_BLOCK, samples), lambda i: (i, 0))
    table = pl.BlockSpec((OUTER, 2 * LANES, 2 * LANES), lambda i: (0, 0, 0), pipeline_mode=once)
    return pl.pallas_call(
        functools.partial(channelize_kernel, step, ants),
        grid=(ants // ANT_BLOCK,),
        in_specs=[
            stream,
            stream,
            pl.BlockSpec((TAPS, FREQ_CHANNELS), lambda i: (0, 0), pipeline_mode=once),
            table,
            table,
        ],
        out_specs=pl.BlockSpec((OUTER, 16, 16, columns), lambda i: (0, 0, 0, 0), pipeline_mode=once),
        out_shape=jax.ShapeDtypeStruct((OUTER, 16, 16, columns), jnp.bfloat16),
        scratch_shapes=[
            pltpu.VMEM((SPECTRA_PER_STEP, 2, OUTER, 8, LANES), jnp.float32),
            pltpu.VMEM((SPECTRA_PER_STEP, 2, OUTER, 8, LANES), jnp.float32),
            pltpu.VMEM((OUTER, columns, 2 * LANES), jnp.float32),
        ],
        compiler_params=pltpu.CompilerParams(vmem_limit_bytes=56 * 2**20),
        cost_estimate=pl.CostEstimate(
            flops=20_000_000_000, bytes_accessed=50_000_000, transcendentals=0
        ),
        name="channelize",
    )(voltage_real, voltage_imaginary, filter_taps, high, low)


def detect_kernel(sources, ants, x_ref, w_ref, out_ref, xs_ref):
    rows = x_ref.shape[1]
    for t in range(SPECTRA_PER_STEP):
        for pair in range(sources // 2):
            xs_ref[t * rows : (t + 1) * rows, 2 * pair * ants : 2 * (pair + 1) * ants] = jnp.concatenate(
                [x_ref[2 * pair + j, :, t * ants : (t + 1) * ants] for j in range(2)], 1
            )
    beams = w_ref.shape[1] // 2
    total = None
    for t in range(SPECTRA_PER_STEP):
        g = jnp.dot(xs_ref[t * rows : (t + 1) * rows], w_ref[...], preferred_element_type=jnp.float32)
        g = g.reshape(rows // 16, 2, 8, 2 * beams)
        re, im = g[:, 0], g[:, 1]
        beam_re = re[..., :beams] - im[..., beams:]
        beam_im = re[..., beams:] + im[..., :beams]
        power = beam_re * beam_re + beam_im * beam_im
        total = power if total is None else total + power
    out_ref[...] = (total * (1.0 / SPECTRA_PER_STEP)).reshape(rows // 2, beams)


def detect(received, weights, sources):
    rows, columns = received.shape[1], received.shape[2]
    ants = columns // SPECTRA_PER_STEP
    beams = weights.shape[1] // 2
    block = rows // 2
    power = pl.pallas_call(
        functools.partial(detect_kernel, sources, ants),
        grid=(2,),
        in_specs=[
            pl.BlockSpec((sources, block, columns), lambda i: (0, i, 0)),
            pl.BlockSpec(weights.shape, lambda i: (0, 0), pipeline_mode=pl.Buffered(1)),
        ],
        out_specs=pl.BlockSpec((block // 2, beams), lambda i: (i, 0)),
        out_shape=jax.ShapeDtypeStruct((rows // 2, beams), jnp.float32),
        scratch_shapes=[pltpu.VMEM((SPECTRA_PER_STEP * block, sources * ants), jnp.bfloat16)],
        compiler_params=pltpu.CompilerParams(vmem_limit_bytes=48 * 2**20),
        cost_estimate=pl.CostEstimate(flops=6_500_000_000, bytes_accessed=11_000_000, transcendentals=0),
        name="detect",
    )(received, weights)
    return power.reshape(OUTER, 4, beams).swapaxes(0, 1).reshape(rows // 2, beams)


def detect_any(received, weights, sources, owned):
    ants = received.shape[-1]
    beams = weights.shape[1] // 2
    rows = received.transpose(4, 1, 3, 5, 2, 0, 6).reshape(
        OUTER * owned, SPECTRA_PER_STEP, 2, sources * ants
    )
    terms = jnp.einsum("ftpa,ab->ftpb", rows, weights, preferred_element_type=jnp.float32)
    beam_re = terms[:, :, 0, :beams] - terms[:, :, 1, beams:]
    beam_im = terms[:, :, 0, beams:] + terms[:, :, 1, :beams]
    return jnp.mean(beam_re**2 + beam_im**2, axis=1)


def on_device(groups, members, vr, vi, filter_taps, weights_re, weights_im, owners, antenna_map):
    devices = groups * members
    ants = vr.shape[0]
    total_ants = antenna_map.shape[0]
    quarter = total_ants // groups
    rows = lax.dynamic_slice_in_dim(antenna_map, lax.axis_index("grp") * quarter, quarter)
    own = jnp.concatenate(
        [
            jnp.take(weights_re[0], rows, axis=0).astype(jnp.bfloat16),
            jnp.take(weights_im[0], rows, axis=0).astype(jnp.bfloat16),
        ],
        1,
    )
    mine = lax.axis_index("dev") == owners
    kept = jnp.where(mine[:, None, None], own[None], 0).astype(jnp.bfloat16)
    kept, filter_taps = lax.optimization_barrier((kept, filter_taps))
    summed = lax.psum(kept, "dev")

    high, low = (jnp.asarray(table) for table in dft_tables())
    owned = LANES // devices
    sent = []
    for step in range(STEPS):
        spectra = channelize(step, vr, vi, filter_taps, high, low)
        if devices != OUTER:
            spectra = spectra.reshape(OUTER, 16, 2, 2, 4 // owned, owned, SPECTRA_PER_STEP * ants)
            spectra = spectra.transpose(0, 4, 1, 2, 3, 5, 6)
        spectra = spectra.reshape(devices, -1, SPECTRA_PER_STEP * ants)
        if step == STEPS - 1:
            spectra, summed = lax.optimization_barrier((spectra, summed))
        sent.append(lax.all_to_all(spectra, ("grp", "dev"), split_axis=0, concat_axis=0, tiled=True))
    weights = lax.all_gather(summed, "grp", axis=1, tiled=True)
    outputs = []
    for step in range(STEPS):
        if devices == OUTER:
            outputs.append(detect(sent[step], weights[step], devices))
        else:
            received = sent[step].reshape(devices, 16, 2, 2, owned, SPECTRA_PER_STEP, ants)
            outputs.append(detect_any(received, weights[step], devices, owned))
    return jnp.stack(outputs)


def solution(mesh):
    groups, members = mesh.shape["grp"], mesh.shape["dev"]
    return jax.shard_map(
        functools.partial(on_device, groups, members),
        mesh=mesh,
        in_specs=(
            P(("grp", "dev"), None),
            P(("grp", "dev"), None),
            P(),
            P("dev", None, None),
            P("dev", None, None),
            P(),
            P(),
        ),
        out_specs=P(None, ("grp", "dev"), None),
        check_vma=False,
    )
```
